32 devices in a mesh: dom: 16 (over z, y, x), off: 2 (over core).
Axes of the slice: x: 2, y: 2, z: 4, core: 2. Of those that a mesh axis runs over, the one named last changes fastest.
Arguments:
- contrib: float32 [384, 2432], P('dom'), may hold values from -6 to 6
- slot_octant: int32 [384], P('dom'), may hold values from 0 to 255, as said below
- vlist_src: int32 [256, 40], P('dom'), may hold values from 0 to 255, as said below
- vlist_class: int32 [256, 40], P('dom'), may hold values from 0 to 79, as said below
- translation: float32 [80, 152, 152], P('off'), may hold values from -0.078125 to 0.078125
Outputs:
- potential: float32 [256, 2432], P(('dom', 'off'))
The draws below stay inside these ranges and needn't reach their ends.
Inputs may be any that keep to these rules, and one draw needn't show every extreme that they name: `slot_octant`: slot k < 16 of partition p names octant p * 16 + k; its other slots name octants p * 16 + j with -4 <= j < 20, taken modulo 256, and each partition has one slot at j = -4 and one at j = 19. vlist_src[t, l] = t + d modulo 256, where the nonzero offset d, with |d| <= 12, depends only on the class vlist_class[t, l]; some class has d = 12 and some d = -12. `vlist_class`: the 40 classes of one octant are all different, and every class is used by some octant.
All inputs are finite; a program needn't handle non-finite values.
Results may differ from the reference program's by a relative error of at most 0.00007.
Values sent between devices are 32-bit elements; how exact they have to be, the bound alone decides.
No kernel may reach another device: no remote copies, remote signals or barrier semaphores. Data moves between devices by JAX's collectives and lax.ppermute only.
A program may use at most 64 MiB of HBM per device.

```python
import jax
import jax.numpy as jnp
from jax import lax

E = 152
R = 16
TGT = 16
SPILL = 4
SLOTS = 24
NOCT = 256
CLS = 80
VL = 40
N_DOM = 16


def draw_slot_octant(key, part):
    row_ids = jnp.arange(N_DOM * SLOTS, dtype=jnp.int32)
    owner = row_ids // SLOTS
    within = row_ids % SLOTS
    spread = jax.random.randint(key, (N_DOM * SLOTS,), -SPILL, TGT + SPILL, dtype=jnp.int32)
    placed = jnp.where(within < TGT, within, spread)
    placed = jnp.where(within == TGT, -SPILL, placed)
    placed = jnp.where(within == TGT + 1, TGT + SPILL - 1, placed)
    return ((owner * TGT + placed + NOCT) % NOCT).astype(jnp.int32)


def vlist_tables(key):
    base = jax.random.fold_in(key, 4099)
    reach = TGT - SPILL
    steps_all = jnp.arange(2 * reach, dtype=jnp.int32)
    signed = (reach - steps_all // 2) * (1 - 2 * (steps_all % 2))
    shuffled = jax.random.permutation(jax.random.fold_in(base, 1), CLS).astype(jnp.int32)
    class_offset = signed[shuffled % (2 * reach)]
    scores = jax.random.randint(jax.random.fold_in(base, 2), (NOCT, CLS), 0, 2 ** 20, dtype=jnp.int32)
    columns = jnp.arange(CLS, dtype=jnp.int32)
    scores = scores * CLS + columns[None, :]
    forced = shuffled[jnp.arange(NOCT, dtype=jnp.int32) % CLS]
    scores = jnp.where(columns[None, :] == forced[:, None], -1, scores)
    classes = jnp.argsort(scores, axis=1)[:, :VL].astype(jnp.int32)
    rows = jnp.arange(NOCT, dtype=jnp.int32)[:, None]
    sources = ((rows + class_offset[classes] + NOCT) % NOCT).astype(jnp.int32)
    return (classes, sources)


def draw_vlist_class(key, part):
    return vlist_tables(key)[0]


def draw_vlist_src(key, part):
    return vlist_tables(key)[1]


def levels(own_key, dims, cuts, low, high):
    def one(axis_at, blocks):
        draws = jax.random.uniform(jax.random.fold_in(jax.random.fold_in(own_key, 6), axis_at), (blocks,), jnp.float32, low / len(cuts), high / len(cuts))
        return jnp.repeat(jnp.exp(draws), dims[axis_at] // blocks).reshape((-1,) + (1,) * (len(dims) - axis_at - 1))

    gain = one(*cuts[0])
    for cut in cuts[1:]:
        gain = gain * one(*cut)
    return gain


def noise(key, extent, width, bound, shards=(), held_as=jnp.bfloat16):
    gain = levels(key, extent, shards, -0.22, 0.18) if shards else 1.0
    entries = jax.random.normal(key, extent, jnp.float32) * width * gain
    return jnp.minimum(jnp.maximum(entries, -bound), bound).astype(held_as)


def setup_inputs(seed: int = 0) -> dict:
    arg_keys = jax.random.split(jax.random.key(seed), 6)
    return {
        "contrib": noise(arg_keys[0], (N_DOM * SLOTS, E * R), 1.0, 6.0, ((0, 16),), jnp.float32),
        "slot_octant": draw_slot_octant(jax.random.fold_in(arg_keys[5], 71), 0),
        "vlist_src": draw_vlist_src(jax.random.fold_in(arg_keys[5], 71), 0),
        "vlist_class": draw_vlist_class(jax.random.fold_in(arg_keys[5], 71), 0),
        "translation": noise(arg_keys[4], (CLS, E, E), (E * VL) ** -0.5, 0.078125, ((0, 2),), jnp.float32),
    }


def reference(contrib, slot_octant, vlist_src, vlist_class, translation):
    densities = jax.ops.segment_sum(contrib, slot_octant, num_segments=NOCT)

    def one_target(row_data):
        sources, classes = row_data
        blocks = translation[classes]
        gathered = densities[sources].reshape(VL, E, R)
        result = jnp.einsum("lij,ljr->ir", blocks, gathered, precision=lax.Precision.HIGHEST)
        return result.reshape(E * R)

    return lax.map(one_target, (vlist_src, vlist_class))
```

```python
import functools

import jax
import jax.numpy as jnp
from jax import lax
from jax.experimental import pallas as pl
from jax.experimental.pallas import tpu as pltpu
from jax.sharding import PartitionSpec as P

TGT = 16
SPILL = 4
LANES = 128
ROWS = 8
BODY = 64
TAIL = 16
HALF = BODY + TAIL
STEPS = 4
WINDOW = 5
VMEM_LIMIT = 48 * 1024 * 1024
f32, bf16, i32 = jnp.float32, jnp.bfloat16, jnp.int32


def swap_blocks(x, width):
    row = lax.broadcasted_iota(i32, (ROWS, LANES), 0)
    lane = lax.broadcasted_iota(i32, (ROWS, LANES), 1)
    take = functools.partial(jnp.take_along_axis, mode="promise_in_bounds")
    x = take(x, (lane - width * row) & (LANES - 1), axis=1)
    x = take(x, (lane // width - row) & (ROWS - 1), axis=0)
    return take(x, (lane + width * row) & (LANES - 1), axis=1)


def chunk_of(half, at):
    body = BODY // ROWS
    return half * body + at if at < body else 2 * body + half * (TAIL // ROWS) + at - body


def table_kernel(width, octants, slot_hbm, contrib_hbm, right_ref, left_ref, table, slot_ref, contrib_ref, sems):
    copies = [
        pltpu.make_async_copy(slot_hbm, slot_ref, sems.at[0]),
        pltpu.make_async_copy(contrib_hbm, contrib_ref, sems.at[1]),
    ]
    for copy in copies:
        copy.start()
    first = lax.axis_index("dom") * TGT - SPILL
    half = lax.rem(lax.axis_index("off"), 2)
    length = contrib_ref.shape[1]
    table[:ROWS] = jnp.zeros((ROWS, table.shape[1]), f32)
    table[ROWS:TGT, length:] = jnp.zeros((ROWS, table.shape[1] - length), f32)
    table[TGT:] = jnp.zeros((ROWS, table.shape[1]), f32)
    for copy in copies:
        copy.wait()
    table[SPILL : SPILL + TGT, :length] = contrib_ref[:TGT, :]
    for slot in range(TGT, contrib_ref.shape[0]):
        row = lax.rem(slot_ref[slot] - first + octants, octants)
        table[pl.ds(row, 1), :length] += contrib_ref[slot : slot + 1, :]
    for chunk in range(HALF // ROWS):
        lanes = pl.ds(pl.multiple_of(chunk_of(half, chunk) * LANES, LANES), LANES)
        rows = slice(ROWS * chunk, ROWS * (chunk + 1))
        for block in range(3):
            piece = swap_blocks(table[ROWS * block : ROWS * (block + 1), lanes], width)
            if block < 2:
                left_ref[rows, LANES * block : LANES * (block + 1)] = piece
            if block >= 1:
                right_ref[rows, LANES * (block - 1) : LANES * block] = piece


def fill_own(width, table, own_ref):
    for half in range(2):
        for chunk in range(HALF // ROWS):
            at = chunk_of(half, chunk)
            for block in range(3):
                piece = table[ROWS * block : ROWS * (block + 1), LANES * at : LANES * (at + 1)]
                rows, lanes = slice(ROWS * chunk, ROWS * (chunk + 1)), slice(LANES * block, LANES * (block + 1))
                own_ref[half, rows, lanes] = swap_blocks(piece, width)


def halves(x):
    high = x.astype(bf16)
    return high, (x - high.astype(f32)).astype(bf16)


def tail_places():
    source = lax.broadcasted_iota(i32, (2 * LANES, 2 * LANES), 0)
    lane = lax.broadcasted_iota(i32, (2 * LANES, 2 * LANES), 1)
    slot = (lane & (LANES - 1)) // TAIL - BODY // TAIL
    point = lane // LANES * TAIL + lane % TAIL
    wanted = jnp.where(slot == 1, LANES + point, point)
    return jnp.where((slot >= 0) & (slot < 3) & (source == wanted), 1.0, 0.0).astype(bf16)


def fetch(block_hbm, block_ref, sem, begin, end):
    here = pl.ds(begin, end - begin)
    return pltpu.make_async_copy(block_hbm.at[here], block_ref.at[here], sem)


def split_blocks(places, begin, end, block_ref, split_ref):
    points = block_ref.shape[1]
    spare = jnp.zeros((points, 2 * LANES - points), f32)
    lower = lax.broadcasted_iota(i32, (points, LANES), 1) < BODY
    for at in range(begin, end):
        high, low = halves(block_ref[at, :, :LANES])
        rest = jnp.concatenate(halves(jnp.concatenate([block_ref[at, :, LANES:], spare], axis=1)), axis=1)
        tails = jnp.dot(rest, places, preferred_element_type=f32).astype(bf16)
        turned = pltpu.roll(low, BODY, 1)
        split_ref[at, 0, :, :LANES] = jnp.where(lower, high, turned)
        split_ref[at, 0, :, LANES:] = jnp.where(lower, high, tails[:, :LANES])
        split_ref[at, 1, :, :LANES] = jnp.where(lower, turned, high)
        split_ref[at, 1, :, LANES:] = jnp.where(lower, pltpu.roll(high, BODY, 1), tails[:, LANES:])


def find_targets(width, octants, src_ref, class_ref, mask_ref, place_ref):
    count, targets = mask_ref.shape[0], src_ref.shape[0]
    first_class = lax.axis_index("off") * count
    first = lax.axis_index("dom") * TGT
    reach = TGT - SPILL
    target = lax.broadcasted_iota(i32, src_ref.shape, 0)
    offset = lax.rem(src_ref[...] - (first + target) + reach + octants, octants)
    named = class_ref[...] - first_class
    known = (named >= 0) & (named < count)
    code = jnp.where(known, named * 32 + offset, -1).astype(f32)
    owner = lax.broadcasted_iota(i32, (targets, targets * width), 1) // width
    spread = (owner == lax.broadcasted_iota(i32, owner.shape, 0)).astype(f32)
    codes = lax.dot_general(
        code, spread, (((0,), (0,)), ((), ())), precision=lax.Precision.HIGHEST, preferred_element_type=f32
    ).astype(i32)
    for at in range(count):
        found = jnp.where((codes >> 5) == at, codes & 31, -1)
        found = jnp.max(found, axis=0, keepdims=True)
        mask_ref[at : at + 1, :] = (found >= 0).astype(f32)
        best = jnp.max(found, axis=1, keepdims=True)
        shift, turns = jnp.maximum(best[0, 0], 0), LANES // width
        place_ref[at] = lax.rem(shift, turns) * WINDOW + lax.div(shift, turns)


def early_share():
    return jnp.clip(STEPS - lax.axis_index("dom") * 3 // 2, 0, STEPS)


def early_kernel(width, bounds, block_hbm, table, sent_ref, split_ref, own_ref, copied_ref, block_ref, sems):
    copied_ref[...] = sent_ref[...]
    share = early_share()
    copies = [fetch(block_hbm, block_ref, sems.at[step], *bounds[step : step + 2]) for step in range(STEPS)]
    for step in range(STEPS):
        pl.when(step < share)(copies[step].start)

    @pl.when(share > 0)
    def _():
        fill_own(width, table, own_ref)
        places = tail_places()
        for step in range(STEPS):

            @pl.when(step < share)
            def _():
                copies[step].wait()
                split_blocks(places, bounds[step], bounds[step + 1], block_ref, split_ref)


def late_kernel(
    width, octants, bounds, src_hbm, class_hbm, block_hbm, table, _split, _own, split_ref, own_ref, mask_ref, place_ref,
    src_ref, class_ref, block_ref, sems, table_sems
):
    share = early_share()
    tables = [
        pltpu.make_async_copy(src_hbm, src_ref, table_sems.at[0]),
        pltpu.make_async_copy(class_hbm, class_ref, table_sems.at[1]),
    ]
    for copy in tables:
        copy.start()
    steps = len(bounds) - 1
    copies = [fetch(block_hbm, block_ref, sems.at[step], *bounds[step : step + 2]) for step in range(steps)]
    for step in range(steps):
        if step < STEPS:
            pl.when(step >= share)(copies[step].start)
        else:
            copies[step].start()
    pl.when(share == 0)(lambda: fill_own(width, table, own_ref))
    for copy in tables:
        copy.wait()
    find_targets(width, octants, src_ref, class_ref, mask_ref, place_ref)
    places = tail_places()
    for step in range(steps):

        def one_step(step=step):
            copies[step].wait()
            split_blocks(places, bounds[step], bounds[step + 1], block_ref, split_ref)

        if step < STEPS:
            pl.when(step >= share)(one_step)
        else:
            one_step()


def edge_kernel(side, sent_ref, own_ref, *refs):
    half = lax.rem(lax.axis_index("off"), 2)
    near = LANES * (1 - side)
    edge_ref = refs[-1]
    own = own_ref[half, :, 2 * LANES * side : 2 * LANES * side + LANES]
    for at in range(0, 2 * LANES, LANES):
        block = sent_ref[:, at : at + LANES]
        edge_ref[:, at : at + LANES] = block + own if at == near else block


def turn_kernel(width, other, side, edge_ref, own_ref, *refs):
    half = lax.rem(lax.axis_index("off") + other, 2)
    shifted = refs[-1]
    blocks = [edge_ref[:, :LANES], edge_ref[:, LANES:]]
    if side == 0:
        blocks.append(own_ref[half, :, LANES : 2 * LANES])
    stacks = [jnp.concatenate(halves(block), axis=0) for block in blocks]
    lane = lax.broadcasted_iota(i32, stacks[0].shape, 1)
    for turn in range(LANES // width):
        tiles = [pltpu.roll(stack, LANES - width * turn, 1) for stack in stacks] if turn else stacks
        kept = lane < LANES - width * turn
        row = turn * WINDOW
        if side == 0:
            shifted[row] = jnp.where(kept, tiles[0], tiles[1]) if turn else tiles[0]
            shifted[row + 1] = jnp.where(kept, tiles[1], tiles[2]) if turn else tiles[1]
            shifted[row + 2] = tiles[2]
        else:
            if turn:
                shifted[row + 2] = jnp.where(kept, shifted[row + 2], tiles[0])
            shifted[row + 3] = jnp.where(kept, tiles[0], tiles[1]) if turn else tiles[0]
            if not turn:
                shifted[row + 4] = tiles[1]


def multiply_kernel(width, other, split_ref, mask_ref, place_ref, shifted, *refs):
    half = lax.rem(lax.axis_index("off") + other, 2)
    points = split_ref.shape[2]
    span = TGT * width
    if other:
        sum_ref, *out_refs = refs
    else:
        (sum_ref,) = refs
    total = sum_ref[...] if other else jnp.zeros((points, span), f32)
    none = jnp.zeros((TAIL, span), bf16)
    for at in range(mask_ref.shape[0]):
        place = place_ref[at]
        here = mask_ref[at : at + 1, :].astype(bf16)
        both = jnp.concatenate([shifted[place], shifted[place + 1]], axis=1) * here
        high, high_tail, low, low_tail = both[:BODY], both[BODY:HALF], both[HALF : HALF + BODY], both[HALF + BODY :]
        depth = [high, high, low, high_tail, high_tail, low_tail, none]
        total += jnp.dot(split_ref[at, half], jnp.concatenate(depth, axis=0), preferred_element_type=f32)
    if not other:
        sum_ref[...] = total
        return
    shares = len(out_refs)
    lanes = span // shares
    me = lax.axis_index("off")
    for step, out_ref in enumerate(out_refs):
        piece = total[:, :lanes]
        for share in range(1, shares):
            mine = lax.rem(me + step, shares) == share
            piece = jnp.where(mine, total[:, share * lanes : (share + 1) * lanes], piece)
        out_ref[...] = piece


def finish_kernel(width, *refs):
    *in_refs, out_ref = refs
    total = in_refs[0][...]
    for ref in in_refs[1:]:
        total += ref[...]
    lanes = total.shape[1]
    if lanes < LANES:
        total = jnp.concatenate([total, jnp.zeros((total.shape[0], LANES - lanes), f32)], axis=1)
    for tile in range(total.shape[1] // LANES):
        rows = slice(ROWS * tile, min(ROWS * (tile + 1), out_ref.shape[0]))
        for chunk in range(total.shape[0] // ROWS):
            piece = total[ROWS * chunk : ROWS * (chunk + 1), LANES * tile : LANES * (tile + 1)]
            piece = swap_blocks(piece, width)
            out_ref[rows, LANES * chunk : LANES * (chunk + 1)] = piece[: rows.stop - rows.start]


def local(contrib, slot_octant, vlist_src, vlist_class, translation):
    count = lax.axis_size("dom")
    shares = lax.axis_size("off")
    octants = TGT * count
    classes, points, _ = translation.shape
    width = contrib.shape[1] // points
    span = TGT * width
    vmem = pl.BlockSpec(memory_space=pltpu.VMEM)
    smem = pl.BlockSpec(memory_space=pltpu.SMEM)
    hbm = pl.BlockSpec(memory_space=pltpu.HBM)
    params = pltpu.CompilerParams(vmem_limit_bytes=VMEM_LIMIT)

    def call(kernel, name, out_shape, in_specs, scratch_shapes=(), **options):
        run = pl.pallas_call(
            kernel,
            out_shape=out_shape,
            in_specs=in_specs,
            out_specs=jax.tree.map(lambda x: smem if x.shape == (classes,) else vmem, out_shape),
            scratch_shapes=scratch_shapes,
            compiler_params=params,
            name=name,
            **options,
        )
        places = [pltpu.VMEM if spec is vmem else pltpu.SMEM if spec is smem else pltpu.HBM for spec in in_specs]
        return lambda *operands: run(*map(pltpu.with_memory_space_constraint, operands, places))

    half_shape = pltpu.VMEM((HALF, span), f32)
    to_right, to_left, table = call(
        functools.partial(table_kernel, width, octants),
        "table",
        [half_shape, half_shape, pltpu.VMEM((TGT + 2 * SPILL, 2 * HALF * width), f32)],
        [hbm] * 2,
        [pltpu.SMEM(slot_octant.shape, i32), pltpu.VMEM(contrib.shape, f32), pltpu.SemaphoreType.DMA((2,))],
    )(slot_octant, contrib)

    forward = [(i, (i + 1) % count) for i in range(count)]
    backward = [(target, source) for source, target in forward]
    low = lax.ppermute(to_right, "dom", forward)

    step = classes * 7 // 40
    bounds = [step * at for at in range(STEPS + 1)]
    bounds += [(bounds[-1] + classes) // 2, classes]
    split_shape = pltpu.VMEM((classes, 2, points, 2 * LANES), bf16)
    own_shape = pltpu.VMEM((2, HALF, 3 * LANES), f32)
    blocks = pltpu.VMEM(translation.shape, f32)
    split, own, to_left = call(
        functools.partial(early_kernel, width, bounds),
        "early",
        [split_shape, own_shape, half_shape],
        [hbm, vmem, vmem],
        [blocks, pltpu.SemaphoreType.DMA((STEPS,))],
    )(translation, table, to_left)
    high = lax.ppermute(to_left, "dom", backward)
    tables = [pltpu.VMEM(vlist_src.shape, i32), pltpu.VMEM(vlist_class.shape, i32)]
    split, own, *facts = call(
        functools.partial(late_kernel, width, octants, bounds),
        "late",
        [split_shape, own_shape, pltpu.VMEM((classes, span), f32), pltpu.SMEM((classes,), i32)],
        [hbm] * 3 + [vmem] * 3,
        tables + [blocks, pltpu.SemaphoreType.DMA((len(bounds) - 1,)), pltpu.SemaphoreType.DMA((2,))],
        input_output_aliases={4: 0, 5: 1},
    )(vlist_src, vlist_class, translation, table, split, own)
    facts.insert(0, split)

    twins = [(i, i ^ 1) for i in range(shares)]
    turned_shape = pltpu.VMEM((LANES // width * WINDOW, 2 * HALF, LANES), bf16)

    def turned(other, side, edge, *before):
        return call(
            functools.partial(turn_kernel, width, other, side),
            ("left" if side == 0 else "right") + "_turns",
            turned_shape,
            [vmem] * (2 + len(before)),
            **({"input_output_aliases": {2: 0}} if before else {}),
        )(edge, own, *before)

    def edge(side, sent, after, spec):
        return call(functools.partial(edge_kernel, side), "edge", half_shape, [vmem] * 2 + [spec])(sent, own, after)

    left = edge(0, low, facts[2], smem)
    left_other = lax.ppermute(left, "off", twins)
    window = turned(0, 0, left)
    right = edge(1, high, window, vmem)
    right_other = lax.ppermute(right, "off", twins)
    window = turned(0, 1, right, window)
    total = call(
        functools.partial(multiply_kernel, width, 0), "first", pltpu.VMEM((points, span), f32), [vmem, vmem, smem, vmem]
    )(*facts, window)
    window = turned(1, 1, right_other, turned(1, 0, left_other))
    shares_out = call(
        functools.partial(multiply_kernel, width, 1),
        "second",
        [pltpu.VMEM((points, span // shares), f32)] * shares,
        [vmem, vmem, smem, vmem, vmem],
    )(*facts, window, total)

    pieces = [shares_out[0]]
    for step in range(1, shares):
        pairs = [(i, (i + step) % shares) for i in range(shares)]
        pieces.append(lax.ppermute(shares_out[step], "off", pairs))
    return call(
        functools.partial(finish_kernel, width),
        "finish",
        jax.ShapeDtypeStruct((TGT // shares, contrib.shape[1]), f32),
        [vmem] * shares,
    )(*pieces)


def solution(mesh):
    return jax.shard_map(
        local,
        mesh=mesh,
        in_specs=(P("dom", None), P("dom"), P("dom", None), P("dom", None), P("off", None, None)),
        out_specs=P(("dom", "off"), None),
        check_vma=False,
    )
```

```python
import functools

import jax
import jax.numpy as jnp
from jax import lax
from jax.experimental import pallas as pl
from jax.experimental.pallas import tpu as pltpu
from jax.sharding import PartitionSpec as P

TGT = 16
SPILL = 4
LANES = 128
ROWS = 8
BODY = 64
TAIL = 16
HALF = BODY + TAIL
STEPS = 4
WINDOW = 5
VMEM_LIMIT = 48 * 1024 * 1024
f32, bf16, i32 = jnp.float32, jnp.bfloat16, jnp.int32


def swap_blocks(x, width):
    row = lax.broadcasted_iota(i32, (ROWS, LANES), 0)
    lane = lax.broadcasted_iota(i32, (ROWS, LANES), 1)
    take = functools.partial(jnp.take_along_axis, mode="promise_in_bounds")
    x = take(x, (lane - width * row) & (LANES - 1), axis=1)
    x = take(x, (lane // width - row) & (ROWS - 1), axis=0)
    return take(x, (lane + width * row) & (LANES - 1), axis=1)


def chunk_of(half, at):
    body = BODY // ROWS
    return half * body + at if at < body else 2 * body + half * (TAIL // ROWS) + at - body


def add_spill(octants, slot_ref, contrib_ref, table):
    first = lax.axis_index("dom") * TGT - SPILL
    for slot in range(TGT, contrib_ref.shape[0]):
        row = lax.rem(slot_ref[slot] - first + octants, octants)
        table[pl.ds(row, 1), :] += contrib_ref[slot : slot + 1, :]


def table_kernel(width, octants, slot_hbm, contrib_hbm, right_ref, left_ref, slot_ref, contrib_ref, table, sems):
    half = lax.rem(lax.axis_index("off"), 2)
    slots = contrib_ref.shape[0]
    body, tail = BODY // ROWS * LANES, TAIL // ROWS * LANES
    last = contrib_hbm.shape[1] - 2 * body - tail
    copies = [pltpu.make_async_copy(slot_hbm, slot_ref, sems.at[0])]
    for row in range(0, slots, ROWS):
        copies.append(
            pltpu.make_async_copy(
                contrib_hbm.at[pl.ds(row, ROWS), pl.ds(pl.multiple_of(half * body, LANES), body)],
                contrib_ref.at[pl.ds(row, ROWS), pl.ds(0, body)],
                sems.at[1 + row // ROWS],
            )
        )
    tails = [
        pltpu.make_async_copy(
            contrib_hbm.at[:, pl.ds(2 * body + side * tail, length)],
            contrib_ref.at[:, pl.ds(body, length)],
            sems.at[1 + slots // ROWS],
        )
        for side, length in enumerate((tail, last))
    ]
    for copy in copies:
        copy.start()
    for side, copy in enumerate(tails):
        pl.when(half == side)(copy.start)
    table[:ROWS] = jnp.zeros((ROWS, table.shape[1]), f32)
    table[TGT:] = jnp.zeros((ROWS, table.shape[1]), f32)

    @pl.when(half == 1)
    def _():
        contrib_ref[:, body + last :] = jnp.zeros((slots, tail - last), f32)

    for copy in copies:
        copy.wait()
    for side, copy in enumerate(tails):
        pl.when(half == side)(copy.wait)
    table[SPILL : SPILL + TGT, :] = contrib_ref[:TGT, :]
    add_spill(octants, slot_ref, contrib_ref, table)
    for chunk in range(HALF // ROWS):
        lanes = slice(LANES * chunk, LANES * (chunk + 1))
        rows = slice(ROWS * chunk, ROWS * (chunk + 1))
        for block in range(3):
            piece = swap_blocks(table[ROWS * block : ROWS * (block + 1), lanes], width)
            if block < 2:
                left_ref[rows, LANES * block : LANES * (block + 1)] = piece
            if block >= 1:
                right_ref[rows, LANES * (block - 1) : LANES * block] = piece


def fetch_own(slot_hbm, contrib_hbm, slot_ref, contrib_ref, _table, sems):
    return [
        pltpu.make_async_copy(slot_hbm, slot_ref, sems.at[0]),
        pltpu.make_async_copy(contrib_hbm, contrib_ref, sems.at[1]),
    ]


def fill_own(width, octants, copies, slot_ref, contrib_ref, table, own_ref):
    for copy in copies:
        copy.wait()
    table[:ROWS] = jnp.zeros((ROWS, table.shape[1]), f32)
    table[TGT:] = jnp.zeros((ROWS, table.shape[1]), f32)
    table[SPILL : SPILL + TGT, :] = contrib_ref[:TGT, :]
    add_spill(octants, slot_ref, contrib_ref, table)
    for half in range(2):
        for chunk in range(HALF // ROWS):
            at = chunk_of(half, chunk)
            rows = slice(ROWS * chunk, ROWS * (chunk + 1))
            for block in range(3):
                lanes = slice(LANES * block, LANES * (block + 1))
                if LANES * at >= table.shape[1]:
                    own_ref[half, rows, lanes] = jnp.zeros((ROWS, LANES), f32)
                    continue
                piece = table[ROWS * block : ROWS * (block + 1), LANES * at : LANES * (at + 1)]
                own_ref[half, rows, lanes] = swap_blocks(piece, width)


def halves(x):
    high = x.astype(bf16)
    return high, (x - high.astype(f32)).astype(bf16)


def tail_places():
    source = lax.broadcasted_iota(i32, (2 * LANES, 2 * LANES), 0)
    lane = lax.broadcasted_iota(i32, (2 * LANES, 2 * LANES), 1)
    slot = (lane & (LANES - 1)) // TAIL - BODY // TAIL
    point = lane // LANES * TAIL + lane % TAIL
    wanted = jnp.where(slot == 1, LANES + point, point)
    return jnp.where((slot >= 0) & (slot < 3) & (source == wanted), 1.0, 0.0).astype(bf16)


def fetch(block_hbm, block_ref, sem, begin, end):
    here = pl.ds(begin, end - begin)
    return pltpu.make_async_copy(block_hbm.at[here], block_ref.at[here], sem)


def split_blocks(places, begin, end, block_ref, split_ref):
    points = block_ref.shape[1]
    spare = jnp.zeros((points, 2 * LANES - points), f32)
    lower = lax.broadcasted_iota(i32, (points, LANES), 1) < BODY
    for at in range(begin, end):
        high, low = halves(block_ref[at, :, :LANES])
        rest = jnp.concatenate(halves(jnp.concatenate([block_ref[at, :, LANES:], spare], axis=1)), axis=1)
        tails = jnp.dot(rest, places, preferred_element_type=f32).astype(bf16)
        turned = pltpu.roll(low, BODY, 1)
        split_ref[at, 0, :, :LANES] = jnp.where(lower, high, turned)
        split_ref[at, 0, :, LANES:] = jnp.where(lower, high, tails[:, :LANES])
        split_ref[at, 1, :, :LANES] = jnp.where(lower, turned, high)
        split_ref[at, 1, :, LANES:] = jnp.where(lower, pltpu.roll(high, BODY, 1), tails[:, LANES:])


def find_targets(width, octants, src_ref, class_ref, mask_ref, place_ref):
    count, targets = mask_ref.shape[0], src_ref.shape[0]
    first_class = lax.axis_index("off") * count
    first = lax.axis_index("dom") * TGT
    reach = TGT - SPILL
    target = lax.broadcasted_iota(i32, src_ref.shape, 0)
    offset = lax.rem(src_ref[...] - (first + target) + reach + octants, octants)
    named = class_ref[...] - first_class
    known = (named >= 0) & (named < count)
    code = jnp.where(known, named * 32 + offset, -1).astype(f32)
    owner = lax.broadcasted_iota(i32, (targets, targets * width), 1) // width
    spread = (owner == lax.broadcasted_iota(i32, owner.shape, 0)).astype(f32)
    codes = lax.dot_general(
        code, spread, (((0,), (0,)), ((), ())), precision=lax.Precision.HIGHEST, preferred_element_type=f32
    ).astype(i32)
    for at in range(count):
        found = jnp.where((codes >> 5) == at, codes & 31, -1)
        found = jnp.max(found, axis=0, keepdims=True)
        mask_ref[at : at + 1, :] = (found >= 0).astype(f32)
        best = jnp.max(found, axis=1, keepdims=True)
        shift, turns = jnp.maximum(best[0, 0], 0), LANES // width
        place_ref[at] = lax.rem(shift, turns) * WINDOW + lax.div(shift, turns)


def early_share():
    return jnp.clip(STEPS - lax.axis_index("dom") * 3 // 2, 0, STEPS)


def early_kernel(
    width, octants, bounds, slot_hbm, contrib_hbm, block_hbm, _sent, split_ref, own_ref, _copied, block_ref, sems, *parts
):
    share = early_share()
    copies = [fetch(block_hbm, block_ref, sems.at[step], *bounds[step : step + 2]) for step in range(STEPS)]
    own_copies = fetch_own(slot_hbm, contrib_hbm, *parts)

    @pl.when(share > 0)
    def _():
        for copy in own_copies:
            copy.start()
        for step in range(STEPS):
            pl.when(step < share)(copies[step].start)
        places = tail_places()
        for step in range(STEPS):

            @pl.when(step < share)
            def _():
                copies[step].wait()
                split_blocks(places, bounds[step], bounds[step + 1], block_ref, split_ref)

        fill_own(width, octants, own_copies, *parts[:3], own_ref)


def late_kernel(
    width, octants, bounds, src_hbm, class_hbm, slot_hbm, contrib_hbm, block_hbm, _split, _own,
    split_ref, own_ref, mask_ref, place_ref, src_ref, class_ref, block_ref, sems, table_sems, *parts
):
    share = early_share()
    tables = [
        pltpu.make_async_copy(src_hbm, src_ref, table_sems.at[0]),
        pltpu.make_async_copy(class_hbm, class_ref, table_sems.at[1]),
    ]
    for copy in tables:
        copy.start()
    own_copies = fetch_own(slot_hbm, contrib_hbm, *parts)
    for copy in own_copies:
        pl.when(share == 0)(copy.start)
    steps = len(bounds) - 1
    copies = [fetch(block_hbm, block_ref, sems.at[step], *bounds[step : step + 2]) for step in range(steps)]
    for step in range(steps):
        if step < STEPS:
            pl.when(step >= share)(copies[step].start)
        else:
            copies[step].start()
    for copy in tables:
        copy.wait()
    find_targets(width, octants, src_ref, class_ref, mask_ref, place_ref)
    places = tail_places()
    for step in range(steps):

        def one_step(step=step):
            copies[step].wait()
            split_blocks(places, bounds[step], bounds[step + 1], block_ref, split_ref)

        if step < STEPS:
            pl.when(step >= share)(one_step)
        else:
            one_step()
    pl.when(share == 0)(lambda: fill_own(width, octants, own_copies, *parts[:3], own_ref))


def edge_kernel(side, sent_ref, own_ref, *refs):
    half = lax.rem(lax.axis_index("off"), 2)
    near = LANES * (1 - side)
    edge_ref = refs[-1]
    own = own_ref[half, :, 2 * LANES * side : 2 * LANES * side + LANES]
    for at in range(0, 2 * LANES, LANES):
        block = sent_ref[:, at : at + LANES]
        edge_ref[:, at : at + LANES] = block + own if at == near else block


def turn(width, half, side, edge_ref, own_ref, shifted):
    blocks = [edge_ref[:, :LANES], edge_ref[:, LANES:]]
    if side == 0:
        blocks.append(own_ref[half, :, LANES : 2 * LANES])
    stacks = [jnp.concatenate(halves(block), axis=0) for block in blocks]
    lane = lax.broadcasted_iota(i32, stacks[0].shape, 1)
    for by in range(LANES // width):
        tiles = [pltpu.roll(stack, LANES - width * by, 1) for stack in stacks] if by else stacks
        kept = lane < LANES - width * by
        row = by * WINDOW
        if side == 0:
            shifted[row] = jnp.where(kept, tiles[0], tiles[1]) if by else tiles[0]
            shifted[row + 1] = jnp.where(kept, tiles[1], tiles[2]) if by else tiles[1]
            shifted[row + 2] = tiles[2]
        else:
            if by:
                shifted[row + 2] = jnp.where(kept, shifted[row + 2], tiles[0])
            shifted[row + 3] = jnp.where(kept, tiles[0], tiles[1]) if by else tiles[0]
            if not by:
                shifted[row + 4] = tiles[1]
        yield


def turn_kernel(width, other, side, edge_ref, own_ref, *refs):
    half = lax.rem(lax.axis_index("off") + other, 2)
    for _ in turn(width, half, side, edge_ref, own_ref, refs[-1]):
        pass


def products(half, begin, end, split_ref, mask_ref, place_ref, shifted, total, beside=()):
    beside = iter(beside)
    none = jnp.zeros((TAIL, total.shape[1]), bf16)
    for at in range(begin, end):
        place = place_ref[at]
        here = mask_ref[at : at + 1, :].astype(bf16)
        both = jnp.concatenate([shifted[place], shifted[place + 1]], axis=1) * here
        high, high_tail, low, low_tail = both[:BODY], both[BODY:HALF], both[HALF : HALF + BODY], both[HALF + BODY :]
        depth = [high, high, low, high_tail, high_tail, low_tail, none]
        total += jnp.dot(split_ref[at, half], jnp.concatenate(depth, axis=0), preferred_element_type=f32)
        if (at - begin) % 2:
            next(beside, None)
    for _ in beside:
        pass
    return total


def first_kernel(begin, end, split_ref, mask_ref, place_ref, shifted, sum_ref):
    half = lax.rem(lax.axis_index("off"), 2)
    total = jnp.zeros(sum_ref.shape, f32)
    sum_ref[...] = products(half, begin, end, split_ref, mask_ref, place_ref, shifted, total)


def beside_kernel(width, begin, end, split_ref, mask_ref, place_ref, shifted, before, edge_ref, own_ref, sum_ref, turned):
    half = lax.rem(lax.axis_index("off"), 2)
    turns = turn(width, 1 - half, 0, edge_ref, own_ref, turned)
    sum_ref[...] = products(half, begin, end, split_ref, mask_ref, place_ref, shifted, before[...], turns)


def second_kernel(split_ref, mask_ref, place_ref, shifted, before, *out_refs):
    me = lax.axis_index("off")
    half = lax.rem(me + 1, 2)
    total = products(half, 0, mask_ref.shape[0], split_ref, mask_ref, place_ref, shifted, before[...])
    shares = len(out_refs)
    lanes = total.shape[1] // shares
    for step, out_ref in enumerate(out_refs):
        piece = total[:, :lanes]
        for share in range(1, shares):
            mine = lax.rem(me + step, shares) == share
            piece = jnp.where(mine, total[:, share * lanes : (share + 1) * lanes], piece)
        out_ref[...] = piece


def finish_kernel(width, *refs):
    *in_refs, out_ref = refs
    total = in_refs[0][...]
    for ref in in_refs[1:]:
        total += ref[...]
    lanes = total.shape[1]
    if lanes < LANES:
        total = jnp.concatenate([total, jnp.zeros((total.shape[0], LANES - lanes), f32)], axis=1)
    for tile in range(total.shape[1] // LANES):
        rows = slice(ROWS * tile, min(ROWS * (tile + 1), out_ref.shape[0]))
        for chunk in range(total.shape[0] // ROWS):
            piece = total[ROWS * chunk : ROWS * (chunk + 1), LANES * tile : LANES * (tile + 1)]
            piece = swap_blocks(piece, width)
            out_ref[rows, LANES * chunk : LANES * (chunk + 1)] = piece[: rows.stop - rows.start]


def local(contrib, slot_octant, vlist_src, vlist_class, translation):
    count = lax.axis_size("dom")
    shares = lax.axis_size("off")
    octants = TGT * count
    classes, points, _ = translation.shape
    width = contrib.shape[1] // points
    span = TGT * width
    vmem = pl.BlockSpec(memory_space=pltpu.VMEM)
    smem = pl.BlockSpec(memory_space=pltpu.SMEM)
    hbm = pl.BlockSpec(memory_space=pltpu.HBM)
    params = pltpu.CompilerParams(vmem_limit_bytes=VMEM_LIMIT)

    def call(kernel, name, out_shape, in_specs, scratch_shapes=(), **options):
        run = pl.pallas_call(
            kernel,
            out_shape=out_shape,
            in_specs=in_specs,
            out_specs=jax.tree.map(lambda x: smem if x.shape == (classes,) else vmem, out_shape),
            scratch_shapes=scratch_shapes,
            compiler_params=params,
            name=name,
            **options,
        )
        places = [pltpu.VMEM if spec is vmem else pltpu.SMEM if spec is smem else pltpu.HBM for spec in in_specs]
        return lambda *operands: run(*map(pltpu.with_memory_space_constraint, operands, places))

    half_shape = pltpu.VMEM((HALF, span), f32)
    slots = slot_octant.shape[0]
    to_right, to_left = call(
        functools.partial(table_kernel, width, octants),
        "table",
        [half_shape, half_shape],
        [hbm] * 2,
        [
            pltpu.SMEM((slots,), i32),
            pltpu.VMEM((slots, HALF * width), f32),
            pltpu.VMEM((TGT + 2 * SPILL, HALF * width), f32),
            pltpu.SemaphoreType.DMA((2 + slots // ROWS,)),
        ],
    )(slot_octant, contrib)

    forward = [(i, (i + 1) % count) for i in range(count)]
    backward = [(target, source) for source, target in forward]
    low = lax.ppermute(to_right, "dom", forward)

    step = classes * 6 // 40
    bounds = [step * at for at in range(STEPS + 1)]
    bounds += [(bounds[-1] + classes) // 2, classes]
    split_shape = pltpu.VMEM((classes, 2, points, 2 * LANES), bf16)
    own_shape = pltpu.VMEM((2, HALF, 3 * LANES), f32)
    blocks = pltpu.VMEM(translation.shape, f32)
    own_parts = [
        pltpu.SMEM((slots,), i32),
        pltpu.VMEM(contrib.shape, f32),
        pltpu.VMEM((TGT + 2 * SPILL, contrib.shape[1]), f32),
        pltpu.SemaphoreType.DMA((2,)),
    ]
    split, own, to_left = call(
        functools.partial(early_kernel, width, octants, bounds),
        "early",
        [split_shape, own_shape, half_shape],
        [hbm] * 3 + [vmem],
        [blocks, pltpu.SemaphoreType.DMA((STEPS,))] + own_parts,
        input_output_aliases={3: 2},
    )(slot_octant, contrib, translation, to_left)
    high = lax.ppermute(to_left, "dom", backward)
    tables = [pltpu.VMEM(vlist_src.shape, i32), pltpu.VMEM(vlist_class.shape, i32)]
    split, own, *facts = call(
        functools.partial(late_kernel, width, octants, bounds),
        "late",
        [split_shape, own_shape, pltpu.VMEM((classes, span), f32), pltpu.SMEM((classes,), i32)],
        [hbm] * 5 + [vmem] * 2,
        tables + [blocks, pltpu.SemaphoreType.DMA((len(bounds) - 1,)), pltpu.SemaphoreType.DMA((2,))] + own_parts,
        input_output_aliases={5: 0, 6: 1},
    )(vlist_src, vlist_class, slot_octant, contrib, translation, split, own)
    facts.insert(0, split)

    twins = [(i, i ^ 1) for i in range(shares)]
    turned_shape = pltpu.VMEM((LANES // width * WINDOW, 2 * HALF, LANES), bf16)

    def turned(other, side, edge, *before):
        return call(
            functools.partial(turn_kernel, width, other, side),
            ("left" if side == 0 else "right") + "_turns",
            turned_shape,
            [vmem] * (2 + len(before)),
            **({"input_output_aliases": {2: 0}} if before else {}),
        )(edge, own, *before)

    def edge(side, sent, after, spec):
        return call(functools.partial(edge_kernel, side), "edge", half_shape, [vmem] * 2 + [spec])(sent, own, after)

    left = edge(0, low, facts[2], smem)
    left_other = lax.ppermute(left, "off", twins)
    window = turned(0, 0, left)
    right = edge(1, high, window, vmem)
    right_other = lax.ppermute(right, "off", twins)
    window = turned(0, 1, right, window)
    sum_shape = pltpu.VMEM((points, span), f32)
    middle = classes // 2
    tables = [vmem, vmem, smem]
    total = call(functools.partial(first_kernel, 0, middle), "first", sum_shape, tables + [vmem])(*facts, window)
    total, window = call(
        functools.partial(beside_kernel, width, middle, classes),
        "first_beside_turns",
        [sum_shape, turned_shape],
        tables + [vmem] * 4,
    )(*facts, window, total, left_other, own)
    window = turned(1, 1, right_other, window)
    shares_out = call(
        second_kernel, "second", [pltpu.VMEM((points, span // shares), f32)] * shares, tables + [vmem] * 2
    )(*facts, window, total)

    pieces = [shares_out[0]]
    for step in range(1, shares):
        pairs = [(i, (i + step) % shares) for i in range(shares)]
        pieces.append(lax.ppermute(shares_out[step], "off", pairs))
    return call(
        functools.partial(finish_kernel, width),
        "finish",
        jax.ShapeDtypeStruct((TGT // shares, contrib.shape[1]), f32),
        [vmem] * shares,
    )(*pieces)


def solution(mesh):
    return jax.shard_map(
        local,
        mesh=mesh,
        in_specs=(P("dom", None), P("dom"), P("dom", None), P("dom", None), P("off", None, None)),
        out_specs=P(("dom", "off"), None),
        check_vma=False,
    )
```

```python
import functools

import jax
import jax.numpy as jnp
from jax import lax
from jax.experimental import pallas as pl
from jax.experimental.pallas import tpu as pltpu
from jax.sharding import PartitionSpec as P

TGT = 16
SPILL = 4
LANES = 128
ROWS = 8
BODY = 64
TAIL = 16
HALF = BODY + TAIL
STEPS = 4
WINDOW = 5
VMEM_LIMIT = 48 * 1024 * 1024
f32, bf16, i32 = jnp.float32, jnp.bfloat16, jnp.int32


def swap_blocks(x, width):
    row = lax.broadcasted_iota(i32, (ROWS, LANES), 0)
    lane = lax.broadcasted_iota(i32, (ROWS, LANES), 1)
    take = functools.partial(jnp.take_along_axis, mode="promise_in_bounds")
    x = take(x, (lane - width * row) & (LANES - 1), axis=1)
    x = take(x, (lane // width - row) & (ROWS - 1), axis=0)
    return take(x, (lane + width * row) & (LANES - 1), axis=1)


def chunk_of(half, at):
    body = BODY // ROWS
    return half * body + at if at < body else 2 * body + half * (TAIL // ROWS) + at - body


def add_spill(octants, slot_ref, contrib_ref, table):
    first = lax.axis_index("dom") * TGT - SPILL
    for slot in range(TGT, contrib_ref.shape[0]):
        row = lax.rem(slot_ref[slot] - first + octants, octants)
        table[pl.ds(row, 1), :] += contrib_ref[slot : slot + 1, :]


def table_kernel(width, octants, slot_hbm, contrib_hbm, right_ref, left_ref, slot_ref, contrib_ref, table, sems):
    half = lax.rem(lax.axis_index("off"), 2)
    slots = contrib_ref.shape[0]
    body, tail = BODY // ROWS * LANES, TAIL // ROWS * LANES
    last = contrib_hbm.shape[1] - 2 * body - tail
    copies = [pltpu.make_async_copy(slot_hbm, slot_ref, sems.at[0])]
    for row in range(0, slots, ROWS):
        copies.append(
            pltpu.make_async_copy(
                contrib_hbm.at[pl.ds(row, ROWS), pl.ds(pl.multiple_of(half * body, LANES), body)],
                contrib_ref.at[pl.ds(row, ROWS), pl.ds(0, body)],
                sems.at[1 + row // ROWS],
            )
        )
    tails = [
        pltpu.make_async_copy(
            contrib_hbm.at[:, pl.ds(2 * body + side * tail, length)],
            contrib_ref.at[:, pl.ds(body, length)],
            sems.at[1 + slots // ROWS],
        )
        for side, length in enumerate((tail, last))
    ]
    for copy in copies:
        copy.start()
    for side, copy in enumerate(tails):
        pl.when(half == side)(copy.start)
    table[:ROWS] = jnp.zeros((ROWS, table.shape[1]), f32)
    table[TGT:] = jnp.zeros((ROWS, table.shape[1]), f32)

    @pl.when(half == 1)
    def _():
        contrib_ref[:, body + last :] = jnp.zeros((slots, tail - last), f32)

    for copy in copies:
        copy.wait()
    for side, copy in enumerate(tails):
        pl.when(half == side)(copy.wait)
    table[SPILL : SPILL + TGT, :] = contrib_ref[:TGT, :]
    add_spill(octants, slot_ref, contrib_ref, table)
    for chunk in range(HALF // ROWS):
        lanes = slice(LANES * chunk, LANES * (chunk + 1))
        rows = slice(ROWS * chunk, ROWS * (chunk + 1))
        for block in range(3):
            piece = swap_blocks(table[ROWS * block : ROWS * (block + 1), lanes], width)
            if block < 2:
                left_ref[rows, LANES * block : LANES * (block + 1)] = piece
            if block >= 1:
                right_ref[rows, LANES * (block - 1) : LANES * block] = piece


def fetch_own(slot_hbm, contrib_hbm, slot_ref, contrib_ref, _table, sems):
    return [
        pltpu.make_async_copy(slot_hbm, slot_ref, sems.at[0]),
        pltpu.make_async_copy(contrib_hbm, contrib_ref, sems.at[1]),
    ]


def fill_own(width, octants, copies, slot_ref, contrib_ref, table, own_ref):
    for copy in copies:
        copy.wait()
    table[:ROWS] = jnp.zeros((ROWS, table.shape[1]), f32)
    table[TGT:] = jnp.zeros((ROWS, table.shape[1]), f32)
    table[SPILL : SPILL + TGT, :] = contrib_ref[:TGT, :]
    add_spill(octants, slot_ref, contrib_ref, table)
    for half in range(2):
        for chunk in range(HALF // ROWS):
            at = chunk_of(half, chunk)
            rows = slice(ROWS * chunk, ROWS * (chunk + 1))
            for block in range(3):
                lanes = slice(LANES * block, LANES * (block + 1))
                if LANES * at >= table.shape[1]:
                    own_ref[half, rows, lanes] = jnp.zeros((ROWS, LANES), f32)
                    continue
                piece = table[ROWS * block : ROWS * (block + 1), LANES * at : LANES * (at + 1)]
                own_ref[half, rows, lanes] = swap_blocks(piece, width)


def halves(x):
    high = x.astype(bf16)
    return high, (x - high.astype(f32)).astype(bf16)


def tail_places():
    source = lax.broadcasted_iota(i32, (2 * LANES, 2 * LANES), 0)
    lane = lax.broadcasted_iota(i32, (2 * LANES, 2 * LANES), 1)
    slot = (lane & (LANES - 1)) // TAIL - BODY // TAIL
    point = lane // LANES * TAIL + lane % TAIL
    wanted = jnp.where(slot == 1, LANES + point, point)
    return jnp.where((slot >= 0) & (slot < 3) & (source == wanted), 1.0, 0.0).astype(bf16)


def fetch(block_hbm, block_ref, sem, begin, end):
    here = pl.ds(begin, end - begin)
    return pltpu.make_async_copy(block_hbm.at[here], block_ref.at[here], sem)


def split_blocks(places, begin, end, block_ref, split_ref):
    points = block_ref.shape[1]
    spare = jnp.zeros((points, 2 * LANES - points), f32)
    lower = lax.broadcasted_iota(i32, (points, LANES), 1) < BODY
    for at in range(begin, end):
        high, low = halves(block_ref[at, :, :LANES])
        rest = jnp.concatenate(halves(jnp.concatenate([block_ref[at, :, LANES:], spare], axis=1)), axis=1)
        tails = jnp.dot(rest, places, preferred_element_type=f32).astype(bf16)
        turned = pltpu.roll(low, BODY, 1)
        split_ref[at, 0, :, :LANES] = jnp.where(lower, high, turned)
        split_ref[at, 0, :, LANES:] = jnp.where(lower, high, tails[:, :LANES])
        split_ref[at, 1, :, :LANES] = jnp.where(lower, turned, high)
        split_ref[at, 1, :, LANES:] = jnp.where(lower, pltpu.roll(high, BODY, 1), tails[:, LANES:])


def find_targets(width, octants, src_ref, class_ref, mask_ref, place_ref):
    count, targets = mask_ref.shape[0], src_ref.shape[0]
    first_class = lax.axis_index("off") * count
    first = lax.axis_index("dom") * TGT
    reach = TGT - SPILL
    target = lax.broadcasted_iota(i32, src_ref.shape, 0)
    offset = lax.rem(src_ref[...] - (first + target) + reach + octants, octants)
    named = class_ref[...] - first_class
    known = (named >= 0) & (named < count)
    code = jnp.where(known, named * 32 + offset, -1).astype(f32)
    owner = lax.broadcasted_iota(i32, (targets, targets * width), 1) // width
    spread = (owner == lax.broadcasted_iota(i32, owner.shape, 0)).astype(f32)
    codes = lax.dot_general(
        code, spread, (((0,), (0,)), ((), ())), precision=lax.Precision.HIGHEST, preferred_element_type=f32
    ).astype(i32)
    for at in range(count):
        found = jnp.where((codes >> 5) == at, codes & 31, -1)
        found = jnp.max(found, axis=0, keepdims=True)
        mask_ref[at : at + 1, :] = (found >= 0).astype(f32)
        best = jnp.max(found, axis=1, keepdims=True)
        shift, turns = jnp.maximum(best[0, 0], 0), LANES // width
        place_ref[at] = lax.rem(shift, turns) * WINDOW + lax.div(shift, turns)


def early_share():
    return jnp.clip(STEPS - lax.axis_index("dom") * 3 // 2, 0, STEPS)


def own_kernel(width, octants, slot_hbm, contrib_hbm, _sent, own_ref, _passed, *parts):
    @pl.when(lax.axis_index("dom") == 0)
    def _():
        own_copies = fetch_own(slot_hbm, contrib_hbm, *parts)
        for copy in own_copies:
            copy.start()
        fill_own(width, octants, own_copies, *parts[:3], own_ref)


def early_kernel(
    width, octants, bounds, slot_hbm, contrib_hbm, block_hbm, _own, _sent, split_ref, own_ref, _passed,
    block_ref, sems, *parts
):
    share = early_share()
    copies = [fetch(block_hbm, block_ref, sems.at[step], *bounds[step : step + 2]) for step in range(STEPS)]
    own_copies = fetch_own(slot_hbm, contrib_hbm, *parts)
    fills = (share > 0) & (lax.axis_index("dom") > 0)

    @pl.when(share > 0)
    def _():
        for copy in own_copies:
            pl.when(fills)(copy.start)
        for step in range(STEPS):
            pl.when(step < share)(copies[step].start)
        places = tail_places()
        for step in range(STEPS):

            @pl.when(step < share)
            def _():
                copies[step].wait()
                split_blocks(places, bounds[step], bounds[step + 1], block_ref, split_ref)

    pl.when(fills)(lambda: fill_own(width, octants, own_copies, *parts[:3], own_ref))


def late_kernel(
    width, octants, bounds, src_hbm, class_hbm, slot_hbm, contrib_hbm, block_hbm, _split, _own,
    split_ref, own_ref, mask_ref, place_ref, src_ref, class_ref, block_ref, sems, table_sems, *parts
):
    share = early_share()
    tables = [
        pltpu.make_async_copy(src_hbm, src_ref, table_sems.at[0]),
        pltpu.make_async_copy(class_hbm, class_ref, table_sems.at[1]),
    ]
    for copy in tables:
        copy.start()
    own_copies = fetch_own(slot_hbm, contrib_hbm, *parts)
    for copy in own_copies:
        pl.when(share == 0)(copy.start)
    steps = len(bounds) - 1
    copies = [fetch(block_hbm, block_ref, sems.at[step], *bounds[step : step + 2]) for step in range(steps)]
    for step in range(steps):
        if step < STEPS:
            pl.when(step >= share)(copies[step].start)
        else:
            copies[step].start()
    for copy in tables:
        copy.wait()
    find_targets(width, octants, src_ref, class_ref, mask_ref, place_ref)
    places = tail_places()
    for step in range(steps):

        def one_step(step=step):
            copies[step].wait()
            split_blocks(places, bounds[step], bounds[step + 1], block_ref, split_ref)

        if step < STEPS:
            pl.when(step >= share)(one_step)
        else:
            one_step()
    pl.when(share == 0)(lambda: fill_own(width, octants, own_copies, *parts[:3], own_ref))


def edge_kernel(sides, own_ref, *refs):
    half = lax.rem(lax.axis_index("off"), 2)
    for at, side in enumerate(sides):
        own = own_ref[half, :, 2 * LANES * side : 2 * LANES * side + LANES]
        for block in range(2):
            lanes = slice(LANES * (2 * at + block), LANES * (2 * at + block + 1))
            sent = refs[at][:, LANES * block : LANES * (block + 1)]
            refs[-1][:, lanes] = sent + own if block == 1 - side else sent


def turn(width, half, side, edge_ref, own_ref, shifted):
    begin = edge_ref.shape[1] - 2 * LANES if side else 0
    blocks = [edge_ref[:, begin : begin + LANES], edge_ref[:, begin + LANES : begin + 2 * LANES]]
    if side == 0:
        blocks.append(own_ref[half, :, LANES : 2 * LANES])
    stacks = [jnp.concatenate(halves(block), axis=0) for block in blocks]
    lane = lax.broadcasted_iota(i32, stacks[0].shape, 1)
    for by in range(LANES // width):
        tiles = [pltpu.roll(stack, LANES - width * by, 1) for stack in stacks] if by else stacks
        kept = lane < LANES - width * by
        row = by * WINDOW
        if side == 0:
            shifted[row] = jnp.where(kept, tiles[0], tiles[1]) if by else tiles[0]
            shifted[row + 1] = jnp.where(kept, tiles[1], tiles[2]) if by else tiles[1]
            shifted[row + 2] = tiles[2]
        else:
            if by:
                shifted[row + 2] = jnp.where(kept, shifted[row + 2], tiles[0])
            shifted[row + 3] = jnp.where(kept, tiles[0], tiles[1]) if by else tiles[0]
            if not by:
                shifted[row + 4] = tiles[1]
        yield


def turn_kernel(width, other, side, edge_ref, own_ref, *refs):
    half = lax.rem(lax.axis_index("off") + other, 2)
    for _ in turn(width, half, side, edge_ref, own_ref, refs[-1]):
        pass


def products(half, begin, end, split_ref, mask_ref, place_ref, shifted, total, beside=()):
    beside = iter(beside)
    none = jnp.zeros((TAIL, total.shape[1]), bf16)
    for at in range(begin, end):
        place = place_ref[at]
        here = mask_ref[at : at + 1, :].astype(bf16)
        both = jnp.concatenate([shifted[place], shifted[place + 1]], axis=1) * here
        high, high_tail, low, low_tail = both[:BODY], both[BODY:HALF], both[HALF : HALF + BODY], both[HALF + BODY :]
        depth = [high, high, low, high_tail, high_tail, low_tail, none]
        total += jnp.dot(split_ref[at, half], jnp.concatenate(depth, axis=0), preferred_element_type=f32)
        if (at - begin) % 2:
            next(beside, None)
    for _ in beside:
        pass
    return total


def first_kernel(begin, end, split_ref, mask_ref, place_ref, shifted, sum_ref):
    half = lax.rem(lax.axis_index("off"), 2)
    total = jnp.zeros(sum_ref.shape, f32)
    sum_ref[...] = products(half, begin, end, split_ref, mask_ref, place_ref, shifted, total)


def second_kernel(split_ref, mask_ref, place_ref, shifted, before, *out_refs):
    me = lax.axis_index("off")
    half = lax.rem(me + 1, 2)
    total = products(half, 0, mask_ref.shape[0], split_ref, mask_ref, place_ref, shifted, before[...])
    shares = len(out_refs)
    lanes = total.shape[1] // shares
    for step, out_ref in enumerate(out_refs):
        piece = total[:, :lanes]
        for share in range(1, shares):
            mine = lax.rem(me + step, shares) == share
            piece = jnp.where(mine, total[:, share * lanes : (share + 1) * lanes], piece)
        out_ref[...] = piece


def finish_kernel(width, *refs):
    *in_refs, out_ref = refs
    total = in_refs[0][...]
    for ref in in_refs[1:]:
        total += ref[...]
    lanes = total.shape[1]
    if lanes < LANES:
        total = jnp.concatenate([total, jnp.zeros((total.shape[0], LANES - lanes), f32)], axis=1)
    for tile in range(total.shape[1] // LANES):
        rows = slice(ROWS * tile, min(ROWS * (tile + 1), out_ref.shape[0]))
        for chunk in range(total.shape[0] // ROWS):
            piece = total[ROWS * chunk : ROWS * (chunk + 1), LANES * tile : LANES * (tile + 1)]
            piece = swap_blocks(piece, width)
            out_ref[rows, LANES * chunk : LANES * (chunk + 1)] = piece[: rows.stop - rows.start]


def local(contrib, slot_octant, vlist_src, vlist_class, translation):
    count = lax.axis_size("dom")
    shares = lax.axis_size("off")
    octants = TGT * count
    classes, points, _ = translation.shape
    width = contrib.shape[1] // points
    span = TGT * width
    vmem = pl.BlockSpec(memory_space=pltpu.VMEM)
    smem = pl.BlockSpec(memory_space=pltpu.SMEM)
    hbm = pl.BlockSpec(memory_space=pltpu.HBM)
    params = pltpu.CompilerParams(vmem_limit_bytes=VMEM_LIMIT)

    def call(kernel, name, out_shape, in_specs, scratch_shapes=(), **options):
        run = pl.pallas_call(
            kernel,
            out_shape=out_shape,
            in_specs=in_specs,
            out_specs=jax.tree.map(lambda x: smem if x.shape == (classes,) else vmem, out_shape),
            scratch_shapes=scratch_shapes,
            compiler_params=params,
            name=name,
            **options,
        )
        places = [pltpu.VMEM if spec is vmem else pltpu.SMEM if spec is smem else pltpu.HBM for spec in in_specs]
        return lambda *operands: run(*map(pltpu.with_memory_space_constraint, operands, places))

    half_shape = pltpu.VMEM((HALF, span), f32)
    slots = slot_octant.shape[0]
    to_right, to_left = call(
        functools.partial(table_kernel, width, octants),
        "table",
        [half_shape, half_shape],
        [hbm] * 2,
        [
            pltpu.SMEM((slots,), i32),
            pltpu.VMEM((slots, HALF * width), f32),
            pltpu.VMEM((TGT + 2 * SPILL, HALF * width), f32),
            pltpu.SemaphoreType.DMA((2 + slots // ROWS,)),
        ],
    )(slot_octant, contrib)

    forward = [(i, (i + 1) % count) for i in range(count)]
    backward = [(target, source) for source, target in forward]
    own_parts = [
        pltpu.SMEM((slots,), i32),
        pltpu.VMEM(contrib.shape, f32),
        pltpu.VMEM((TGT + 2 * SPILL, contrib.shape[1]), f32),
        pltpu.SemaphoreType.DMA((2,)),
    ]
    own_shape = pltpu.VMEM((2, HALF, 3 * LANES), f32)
    own, to_right = call(
        functools.partial(own_kernel, width, octants),
        "own",
        [own_shape, half_shape],
        [hbm] * 2 + [vmem],
        own_parts,
        input_output_aliases={2: 1},
    )(slot_octant, contrib, to_right)
    low = lax.ppermute(to_right, "dom", forward)

    step = classes * 5 // 40
    bounds = [step * at for at in range(STEPS + 1)]
    bounds += [(bounds[-1] + classes) // 2, classes]
    split_shape = pltpu.VMEM((classes, 2, points, 2 * LANES), bf16)
    blocks = pltpu.VMEM(translation.shape, f32)
    split, own, to_left = call(
        functools.partial(early_kernel, width, octants, bounds),
        "early",
        [split_shape, own_shape, half_shape],
        [hbm] * 3 + [vmem] * 2,
        [blocks, pltpu.SemaphoreType.DMA((STEPS,))] + own_parts,
        input_output_aliases={3: 1, 4: 2},
    )(slot_octant, contrib, translation, own, to_left)
    high = lax.ppermute(to_left, "dom", backward)
    tables = [pltpu.VMEM(vlist_src.shape, i32), pltpu.VMEM(vlist_class.shape, i32)]
    split, own, *facts = call(
        functools.partial(late_kernel, width, octants, bounds),
        "late",
        [split_shape, own_shape, pltpu.VMEM((classes, span), f32), pltpu.SMEM((classes,), i32)],
        [hbm] * 5 + [vmem] * 2,
        tables + [blocks, pltpu.SemaphoreType.DMA((len(bounds) - 1,)), pltpu.SemaphoreType.DMA((2,))] + own_parts,
        input_output_aliases={5: 0, 6: 1},
    )(vlist_src, vlist_class, slot_octant, contrib, translation, split, own)
    facts.insert(0, split)

    twins = [(i, i ^ 1) for i in range(shares)]
    turned_shape = pltpu.VMEM((LANES // width * WINDOW, 2 * HALF, LANES), bf16)

    def turned(other, side, edge, *before):
        return call(
            functools.partial(turn_kernel, width, other, side),
            ("left" if side == 0 else "right") + "_turns",
            turned_shape,
            [vmem] * (2 + len(before)),
            **({"input_output_aliases": {2: 0}} if before else {}),
        )(edge, own, *before)

    left = call(functools.partial(edge_kernel, [0]), "edge", half_shape, [vmem, vmem, smem])(own, low, facts[2])
    window = turned(0, 0, left)
    edges = call(
        functools.partial(edge_kernel, [0, 1]), "edges", pltpu.VMEM((HALF, 4 * LANES), f32), [vmem] * 4
    )(own, low, high, window)
    edges_other = lax.ppermute(edges, "off", twins)
    window = turned(0, 1, edges, window)
    sum_shape = pltpu.VMEM((points, span), f32)
    tables = [vmem, vmem, smem]
    total = call(functools.partial(first_kernel, 0, classes), "first", sum_shape, tables + [vmem])(*facts, window)
    window = turned(1, 1, edges_other, turned(1, 0, edges_other))
    shares_out = call(
        second_kernel, "second", [pltpu.VMEM((points, span // shares), f32)] * shares, tables + [vmem] * 2
    )(*facts, window, total)

    pieces = [shares_out[0]]
    for step in range(1, shares):
        pairs = [(i, (i + step) % shares) for i in range(shares)]
        pieces.append(lax.ppermute(shares_out[step], "off", pairs))
    return call(
        functools.partial(finish_kernel, width),
        "finish",
        jax.ShapeDtypeStruct((TGT // shares, contrib.shape[1]), f32),
        [vmem] * shares,
    )(*pieces)


def solution(mesh):
    return jax.shard_map(
        local,
        mesh=mesh,
        in_specs=(P("dom", None), P("dom"), P("dom", None), P("dom", None), P("off", None, None)),
        out_specs=P(("dom", "off"), None),
        check_vma=False,
    )
```

```python
import functools

import jax
import jax.numpy as jnp
from jax import lax
from jax.experimental import pallas as pl
from jax.experimental.pallas import tpu as pltpu
from jax.sharding import PartitionSpec as P

TGT = 16
SPILL = 4
LANES = 128
ROWS = 8
BODY = 64
TAIL = 16
HALF = BODY + TAIL
STEPS = 4
WINDOW = 5
VMEM_LIMIT = 48 * 1024 * 1024
f32, bf16, i32 = jnp.float32, jnp.bfloat16, jnp.int32


def swap_blocks(x, width):
    row = lax.broadcasted_iota(i32, (ROWS, LANES), 0)
    lane = lax.broadcasted_iota(i32, (ROWS, LANES), 1)
    take = functools.partial(jnp.take_along_axis, mode="promise_in_bounds")
    x = take(x, (lane - width * row) & (LANES - 1), axis=1)
    x = take(x, (lane // width - row) & (ROWS - 1), axis=0)
    return take(x, (lane + width * row) & (LANES - 1), axis=1)


def chunk_of(half, at):
    body = BODY // ROWS
    return half * body + at if at < body else 2 * body + half * (TAIL // ROWS) + at - body


def add_spill(octants, slot_ref, contrib_ref, table):
    first = lax.axis_index("dom") * TGT - SPILL
    for slot in range(TGT, contrib_ref.shape[0]):
        row = lax.rem(slot_ref[slot] - first + octants, octants)
        table[pl.ds(row, 1), :] += contrib_ref[slot : slot + 1, :]


def table_kernel(width, octants, slot_hbm, contrib_hbm, right_ref, left_ref, slot_ref, contrib_ref, table, sems):
    half = lax.rem(lax.axis_index("off"), 2)
    slots = contrib_ref.shape[0]
    body, tail = BODY // ROWS * LANES, TAIL // ROWS * LANES
    last = contrib_hbm.shape[1] - 2 * body - tail
    copies = [pltpu.make_async_copy(slot_hbm, slot_ref, sems.at[0])]
    for row in range(0, slots, ROWS):
        copies.append(
            pltpu.make_async_copy(
                contrib_hbm.at[pl.ds(row, ROWS), pl.ds(pl.multiple_of(half * body, LANES), body)],
                contrib_ref.at[pl.ds(row, ROWS), pl.ds(0, body)],
                sems.at[1 + row // ROWS],
            )
        )
    tails = [
        pltpu.make_async_copy(
            contrib_hbm.at[:, pl.ds(2 * body + side * tail, length)],
            contrib_ref.at[:, pl.ds(body, length)],
            sems.at[1 + slots // ROWS],
        )
        for side, length in enumerate((tail, last))
    ]
    for copy in copies:
        copy.start()
    for side, copy in enumerate(tails):
        pl.when(half == side)(copy.start)
    table[:ROWS] = jnp.zeros((ROWS, table.shape[1]), f32)
    table[TGT:] = jnp.zeros((ROWS, table.shape[1]), f32)

    @pl.when(half == 1)
    def _():
        contrib_ref[:, body + last :] = jnp.zeros((slots, tail - last), f32)

    for copy in copies:
        copy.wait()
    for side, copy in enumerate(tails):
        pl.when(half == side)(copy.wait)
    table[SPILL : SPILL + TGT, :] = contrib_ref[:TGT, :]
    add_spill(octants, slot_ref, contrib_ref, table)
    for chunk in range(HALF // ROWS):
        lanes = slice(LANES * chunk, LANES * (chunk + 1))
        rows = slice(ROWS * chunk, ROWS * (chunk + 1))
        for block in range(3):
            piece = swap_blocks(table[ROWS * block : ROWS * (block + 1), lanes], width)
            if block < 2:
                left_ref[rows, LANES * block : LANES * (block + 1)] = piece
            if block >= 1:
                right_ref[rows, LANES * (block - 1) : LANES * block] = piece


def fetch_own(slot_hbm, contrib_hbm, slot_ref, contrib_ref, _table, sems):
    return [
        pltpu.make_async_copy(slot_hbm, slot_ref, sems.at[0]),
        pltpu.make_async_copy(contrib_hbm, contrib_ref, sems.at[1]),
    ]


def fill_own(width, octants, copies, slot_ref, contrib_ref, table, own_ref):
    for copy in copies:
        copy.wait()
    table[:ROWS] = jnp.zeros((ROWS, table.shape[1]), f32)
    table[TGT:] = jnp.zeros((ROWS, table.shape[1]), f32)
    table[SPILL : SPILL + TGT, :] = contrib_ref[:TGT, :]
    add_spill(octants, slot_ref, contrib_ref, table)
    for half in range(2):
        for chunk in range(HALF // ROWS):
            at = chunk_of(half, chunk)
            rows = slice(ROWS * chunk, ROWS * (chunk + 1))
            for block in range(3):
                lanes = slice(LANES * block, LANES * (block + 1))
                if LANES * at >= table.shape[1]:
                    own_ref[half, rows, lanes] = jnp.zeros((ROWS, LANES), f32)
                    continue
                piece = table[ROWS * block : ROWS * (block + 1), LANES * at : LANES * (at + 1)]
                own_ref[half, rows, lanes] = swap_blocks(piece, width)


def halves(x):
    high = x.astype(bf16)
    return high, (x - high.astype(f32)).astype(bf16)


def tail_places():
    source = lax.broadcasted_iota(i32, (2 * LANES, 2 * LANES), 0)
    lane = lax.broadcasted_iota(i32, (2 * LANES, 2 * LANES), 1)
    slot = (lane & (LANES - 1)) // TAIL - BODY // TAIL
    point = lane // LANES * TAIL + lane % TAIL
    wanted = jnp.where(slot == 1, LANES + point, point)
    return jnp.where((slot >= 0) & (slot < 3) & (source == wanted), 1.0, 0.0).astype(bf16)


def fetch(block_hbm, block_ref, sem, begin, end):
    here = pl.ds(begin, end - begin)
    return pltpu.make_async_copy(block_hbm.at[here], block_ref.at[here], sem)


def split_blocks(places, begin, end, block_ref, split_ref):
    points = block_ref.shape[1]
    spare = jnp.zeros((points, 2 * LANES - points), f32)
    lower = lax.broadcasted_iota(i32, (points, LANES), 1) < BODY
    for at in range(begin, end):
        high, low = halves(block_ref[at, :, :LANES])
        rest = jnp.concatenate(halves(jnp.concatenate([block_ref[at, :, LANES:], spare], axis=1)), axis=1)
        tails = jnp.dot(rest, places, preferred_element_type=f32).astype(bf16)
        turned = pltpu.roll(low, BODY, 1)
        split_ref[at, 0, :, :LANES] = jnp.where(lower, high, turned)
        split_ref[at, 0, :, LANES:] = jnp.where(lower, high, tails[:, :LANES])
        split_ref[at, 1, :, :LANES] = jnp.where(lower, turned, high)
        split_ref[at, 1, :, LANES:] = jnp.where(lower, pltpu.roll(high, BODY, 1), tails[:, LANES:])


def find_targets(width, octants, src_ref, class_ref, mask_ref, place_ref):
    count, targets = mask_ref.shape[0], src_ref.shape[0]
    first_class = lax.axis_index("off") * count
    first = lax.axis_index("dom") * TGT
    reach = TGT - SPILL
    target = lax.broadcasted_iota(i32, src_ref.shape, 0)
    offset = lax.rem(src_ref[...] - (first + target) + reach + octants, octants)
    named = class_ref[...] - first_class
    known = (named >= 0) & (named < count)
    code = jnp.where(known, named * 32 + offset, -1).astype(f32)
    owner = lax.broadcasted_iota(i32, (targets, targets * width), 1) // width
    spread = (owner == lax.broadcasted_iota(i32, owner.shape, 0)).astype(f32)
    codes = lax.dot_general(
        code, spread, (((0,), (0,)), ((), ())), precision=lax.Precision.HIGHEST, preferred_element_type=f32
    ).astype(i32)
    for at in range(count):
        found = jnp.where((codes >> 5) == at, codes & 31, -1)
        found = jnp.max(found, axis=0, keepdims=True)
        mask_ref[at : at + 1, :] = (found >= 0).astype(f32)
        best = jnp.max(found, axis=1, keepdims=True)
        shift, turns = jnp.maximum(best[0, 0], 0), LANES // width
        place_ref[at] = lax.rem(shift, turns) * WINDOW + lax.div(shift, turns)


def early_share():
    return jnp.clip(STEPS - lax.axis_index("dom") * 3 // 2, 0, STEPS)


def own_kernel(width, octants, slot_hbm, contrib_hbm, _sent, own_ref, _passed, *parts):
    @pl.when(lax.axis_index("dom") == 0)
    def _():
        own_copies = fetch_own(slot_hbm, contrib_hbm, *parts)
        for copy in own_copies:
            copy.start()
        fill_own(width, octants, own_copies, *parts[:3], own_ref)


def early_kernel(
    width, octants, bounds, slot_hbm, contrib_hbm, block_hbm, _own, _sent, split_ref, own_ref, _passed,
    block_ref, sems, *parts
):
    share = early_share()
    copies = [fetch(block_hbm, block_ref, sems.at[step], *bounds[step : step + 2]) for step in range(STEPS)]
    own_copies = fetch_own(slot_hbm, contrib_hbm, *parts)
    fills = (share > 0) & (lax.axis_index("dom") > 0)

    @pl.when(share > 0)
    def _():
        for copy in own_copies:
            pl.when(fills)(copy.start)
        for step in range(STEPS):
            pl.when(step < share)(copies[step].start)
        places = tail_places()
        for step in range(STEPS):

            @pl.when(step < share)
            def _():
                copies[step].wait()
                split_blocks(places, bounds[step], bounds[step + 1], block_ref, split_ref)

    pl.when(fills)(lambda: fill_own(width, octants, own_copies, *parts[:3], own_ref))


def late_kernel(
    width, octants, bounds, src_hbm, class_hbm, slot_hbm, contrib_hbm, block_hbm, _split, _own,
    split_ref, own_ref, mask_ref, place_ref, src_ref, class_ref, block_ref, sems, table_sems, *parts
):
    share = early_share()
    tables = [
        pltpu.make_async_copy(src_hbm, src_ref, table_sems.at[0]),
        pltpu.make_async_copy(class_hbm, class_ref, table_sems.at[1]),
    ]
    for copy in tables:
        copy.start()
    own_copies = fetch_own(slot_hbm, contrib_hbm, *parts)
    for copy in own_copies:
        pl.when(share == 0)(copy.start)
    steps = len(bounds) - 1
    copies = [fetch(block_hbm, block_ref, sems.at[step], *bounds[step : step + 2]) for step in range(steps)]
    for step in range(steps):
        if step < STEPS:
            pl.when(step >= share)(copies[step].start)
        else:
            copies[step].start()
    for copy in tables:
        copy.wait()
    find_targets(width, octants, src_ref, class_ref, mask_ref, place_ref)
    places = tail_places()
    for step in range(steps):

        def one_step(step=step):
            copies[step].wait()
            split_blocks(places, bounds[step], bounds[step + 1], block_ref, split_ref)

        if step < STEPS:
            pl.when(step >= share)(one_step)
        else:
            one_step()
    pl.when(share == 0)(lambda: fill_own(width, octants, own_copies, *parts[:3], own_ref))


def edge_kernel(sides, own_ref, *refs):
    half = lax.rem(lax.axis_index("off"), 2)
    for at, side in enumerate(sides):
        own = own_ref[half, :, 2 * LANES * side : 2 * LANES * side + LANES]
        for block in range(2):
            lanes = slice(LANES * (2 * at + block), LANES * (2 * at + block + 1))
            sent = refs[at][:, LANES * block : LANES * (block + 1)]
            refs[-1][:, lanes] = sent + own if block == 1 - side else sent


def turn(width, half, side, edge_ref, own_ref, shifted):
    begin = edge_ref.shape[1] - 2 * LANES if side else 0
    blocks = [edge_ref[:, begin : begin + LANES], edge_ref[:, begin + LANES : begin + 2 * LANES]]
    if side == 0:
        blocks.append(own_ref[half, :, LANES : 2 * LANES])
    stacks = [jnp.concatenate(halves(block), axis=0) for block in blocks]
    lane = lax.broadcasted_iota(i32, stacks[0].shape, 1)
    for by in range(LANES // width):
        tiles = [pltpu.roll(stack, LANES - width * by, 1) for stack in stacks] if by else stacks
        kept = lane < LANES - width * by
        row = by * WINDOW
        if side == 0:
            shifted[row] = jnp.where(kept, tiles[0], tiles[1]) if by else tiles[0]
            shifted[row + 1] = jnp.where(kept, tiles[1], tiles[2]) if by else tiles[1]
            shifted[row + 2] = tiles[2]
        else:
            if by:
                shifted[row + 2] = jnp.where(kept, shifted[row + 2], tiles[0])
            shifted[row + 3] = jnp.where(kept, tiles[0], tiles[1]) if by else tiles[0]
            if not by:
                shifted[row + 4] = tiles[1]
        yield


def turn_kernel(width, other, sides, edge_ref, own_ref, *refs):
    half = lax.rem(lax.axis_index("off") + other, 2)
    for _ in zip(*[turn(width, half, side, edge_ref, own_ref, refs[-1]) for side in sides]):
        pass


def products(half, begin, end, split_ref, mask_ref, place_ref, shifted, total, beside=()):
    beside = iter(beside)
    none = jnp.zeros((TAIL, total.shape[1]), bf16)
    for at in range(begin, end):
        place = place_ref[at]
        here = mask_ref[at : at + 1, :].astype(bf16)
        both = jnp.concatenate([shifted[place], shifted[place + 1]], axis=1) * here
        high, high_tail, low, low_tail = both[:BODY], both[BODY:HALF], both[HALF : HALF + BODY], both[HALF + BODY :]
        depth = [high, high, low, high_tail, high_tail, low_tail, none]
        total += jnp.dot(split_ref[at, half], jnp.concatenate(depth, axis=0), preferred_element_type=f32)
        if (at - begin) % 2:
            next(beside, None)
    for _ in beside:
        pass
    return total


def first_kernel(begin, end, split_ref, mask_ref, place_ref, shifted, sum_ref):
    half = lax.rem(lax.axis_index("off"), 2)
    total = jnp.zeros(sum_ref.shape, f32)
    sum_ref[...] = products(half, begin, end, split_ref, mask_ref, place_ref, shifted, total)


def second_kernel(split_ref, mask_ref, place_ref, shifted, before, *out_refs):
    me = lax.axis_index("off")
    half = lax.rem(me + 1, 2)
    total = products(half, 0, mask_ref.shape[0], split_ref, mask_ref, place_ref, shifted, before[...])
    shares = len(out_refs)
    lanes = total.shape[1] // shares
    for step, out_ref in enumerate(out_refs):
        piece = total[:, :lanes]
        for share in range(1, shares):
            mine = lax.rem(me + step, shares) == share
            piece = jnp.where(mine, total[:, share * lanes : (share + 1) * lanes], piece)
        out_ref[...] = piece


def finish_kernel(width, *refs):
    *in_refs, out_ref = refs
    total = in_refs[0][...]
    for ref in in_refs[1:]:
        total += ref[...]
    lanes = total.shape[1]
    if lanes < LANES:
        total = jnp.concatenate([total, jnp.zeros((total.shape[0], LANES - lanes), f32)], axis=1)
    for tile in range(total.shape[1] // LANES):
        rows = slice(ROWS * tile, min(ROWS * (tile + 1), out_ref.shape[0]))
        for chunk in range(total.shape[0] // ROWS):
            piece = total[ROWS * chunk : ROWS * (chunk + 1), LANES * tile : LANES * (tile + 1)]
            piece = swap_blocks(piece, width)
            out_ref[rows, LANES * chunk : LANES * (chunk + 1)] = piece[: rows.stop - rows.start]


def local(contrib, slot_octant, vlist_src, vlist_class, translation):
    count = lax.axis_size("dom")
    shares = lax.axis_size("off")
    octants = TGT * count
    classes, points, _ = translation.shape
    width = contrib.shape[1] // points
    span = TGT * width
    vmem = pl.BlockSpec(memory_space=pltpu.VMEM)
    smem = pl.BlockSpec(memory_space=pltpu.SMEM)
    hbm = pl.BlockSpec(memory_space=pltpu.HBM)
    params = pltpu.CompilerParams(vmem_limit_bytes=VMEM_LIMIT)

    def call(kernel, name, out_shape, in_specs, scratch_shapes=(), **options):
        run = pl.pallas_call(
            kernel,
            out_shape=out_shape,
            in_specs=in_specs,
            out_specs=jax.tree.map(lambda x: smem if x.shape == (classes,) else vmem, out_shape),
            scratch_shapes=scratch_shapes,
            compiler_params=params,
            name=name,
            **options,
        )
        places = [pltpu.VMEM if spec is vmem else pltpu.SMEM if spec is smem else pltpu.HBM for spec in in_specs]
        return lambda *operands: run(*map(pltpu.with_memory_space_constraint, operands, places))

    half_shape = pltpu.VMEM((HALF, span), f32)
    slots = slot_octant.shape[0]
    to_right, to_left = call(
        functools.partial(table_kernel, width, octants),
        "table",
        [half_shape, half_shape],
        [hbm] * 2,
        [
            pltpu.SMEM((slots,), i32),
            pltpu.VMEM((slots, HALF * width), f32),
            pltpu.VMEM((TGT + 2 * SPILL, HALF * width), f32),
            pltpu.SemaphoreType.DMA((2 + slots // ROWS,)),
        ],
    )(slot_octant, contrib)

    forward = [(i, (i + 1) % count) for i in range(count)]
    backward = [(target, source) for source, target in forward]
    own_parts = [
        pltpu.SMEM((slots,), i32),
        pltpu.VMEM(contrib.shape, f32),
        pltpu.VMEM((TGT + 2 * SPILL, contrib.shape[1]), f32),
        pltpu.SemaphoreType.DMA((2,)),
    ]
    own_shape = pltpu.VMEM((2, HALF, 3 * LANES), f32)
    own, to_right = call(
        functools.partial(own_kernel, width, octants),
        "own",
        [own_shape, half_shape],
        [hbm] * 2 + [vmem],
        own_parts,
        input_output_aliases={2: 1},
    )(slot_octant, contrib, to_right)
    low = lax.ppermute(to_right, "dom", forward)

    step = classes * 5 // 40
    bounds = [step * at for at in range(STEPS + 1)]
    bounds += [(bounds[-1] + classes) // 2, classes]
    split_shape = pltpu.VMEM((classes, 2, points, 2 * LANES), bf16)
    blocks = pltpu.VMEM(translation.shape, f32)
    split, own, to_left = call(
        functools.partial(early_kernel, width, octants, bounds),
        "early",
        [split_shape, own_shape, half_shape],
        [hbm] * 3 + [vmem] * 2,
        [blocks, pltpu.SemaphoreType.DMA((STEPS,))] + own_parts,
        input_output_aliases={3: 1, 4: 2},
    )(slot_octant, contrib, translation, own, to_left)
    high = lax.ppermute(to_left, "dom", backward)
    tables = [pltpu.VMEM(vlist_src.shape, i32), pltpu.VMEM(vlist_class.shape, i32)]
    split, own, *facts = call(
        functools.partial(late_kernel, width, octants, bounds),
        "late",
        [split_shape, own_shape, pltpu.VMEM((classes, span), f32), pltpu.SMEM((classes,), i32)],
        [hbm] * 5 + [vmem] * 2,
        tables + [blocks, pltpu.SemaphoreType.DMA((len(bounds) - 1,)), pltpu.SemaphoreType.DMA((2,))] + own_parts,
        input_output_aliases={5: 0, 6: 1},
    )(vlist_src, vlist_class, slot_octant, contrib, translation, split, own)
    facts.insert(0, split)

    twins = [(i, i ^ 1) for i in range(shares)]
    turned_shape = pltpu.VMEM((LANES // width * WINDOW, 2 * HALF, LANES), bf16)

    def turned(other, sides, edge, *before):
        return call(
            functools.partial(turn_kernel, width, other, sides),
            "turns",
            turned_shape,
            [vmem] * (2 + len(before)),
            **({"input_output_aliases": {2: 0}} if before else {}),
        )(edge, own, *before)

    left = call(functools.partial(edge_kernel, [0]), "edge", half_shape, [vmem, vmem, smem])(own, low, facts[2])
    window = turned(0, [0], left)
    edges = call(
        functools.partial(edge_kernel, [0, 1]), "edges", pltpu.VMEM((HALF, 4 * LANES), f32), [vmem] * 4
    )(own, low, high, window)
    edges_other = lax.ppermute(edges, "off", twins)
    window = turned(0, [1], edges, window)
    sum_shape = pltpu.VMEM((points, span), f32)
    tables = [vmem, vmem, smem]
    total = call(functools.partial(first_kernel, 0, classes), "first", sum_shape, tables + [vmem])(*facts, window)
    window = turned(1, [0, 1], edges_other)
    shares_out = call(
        second_kernel, "second", [pltpu.VMEM((points, span // shares), f32)] * shares, tables + [vmem] * 2
    )(*facts, window, total)

    pieces = [shares_out[0]]
    for step in range(1, shares):
        pairs = [(i, (i + step) % shares) for i in range(shares)]
        pieces.append(lax.ppermute(shares_out[step], "off", pairs))
    return call(
        functools.partial(finish_kernel, width),
        "finish",
        jax.ShapeDtypeStruct((TGT // shares, contrib.shape[1]), f32),
        [vmem] * shares,
    )(*pieces)


def solution(mesh):
    return jax.shard_map(
        local,
        mesh=mesh,
        in_specs=(P("dom", None), P("dom"), P("dom", None), P("dom", None), P("off", None, None)),
        out_specs=P(("dom", "off"), None),
        check_vma=False,
    )
```
